256 devices in a mesh: band: 32 (over x, y, core), field: 8 (over z).
Axes of the slice: x: 4, y: 4, z: 8, core: 2. Of those that a mesh axis runs over, the one named last changes fastest.
Arguments:
- column_state: bfloat16 [512, 1280, 256], P(('band', 'field')), may hold values from -6 to 6
- cosine: float32 [512, 1280], P(('band', 'field')), may hold values from 0.2 to 1
- sunlit: int32 [512, 1280], P(('band', 'field')), may hold values from 0 to 1, as said below
- w_in: bfloat16 [256, 2048], replicated, may hold values from -0.375 to 0.375
- w_out: bfloat16 [2048, 128], replicated, may hold values from -0.125 to 0.125
- w_long: bfloat16 [256, 128], replicated, may hold values from -0.375 to 0.375
- fourier: bfloat16 [512, 32, 2, 4, 128], P('band', None, None, None, 'field'), may hold values from -6 to 6
- quadrature: float32 [512], P('band'), may hold values from 0.5 to 2
- legendre: bfloat16 [32, 640, 512], P('band'), may hold values from -0.25 to 0.25
- damping: float32 [32, 640], P('band'), may hold values from 0.1 to 1
Outputs:
- heating: bfloat16 [512, 1280, 128], P(('band', 'field'))
- updated: bfloat16 [512, 32, 2, 4, 128], P('band', None, None, None, 'field')
The draws below stay inside these ranges and needn't reach their ends.
Inputs may be any that keep to these rules, and one draw needn't show every extreme that they name: Sunlit columns form whole blocks of 32 columns along a latitude. Latitude rows come north then south, each ordered from the pole; row r and row r + 256 have 40 sunlit blocks together.
All inputs are finite; a program needn't handle non-finite values.
Results may differ from the reference program's by a relative error of at most 0.0055.
Values may be sent and summed in bfloat16 or wider, within the bound.
A program may use at most 64 MiB of HBM per device.

```python
import math
import jax
import jax.numpy as jnp
from jax import lax

ROWS_DEV = 2
LEV = 128
NDEG = 640
HID = 2048
BCOL = 32
LON = 1280
M_WIN = 32
BLK_ROW = 40
LAT = 512


def draw_sunlit(key, part):
    key = jax.random.fold_in(key, 7)
    key_days, key_start = jax.random.split(key)
    half_rows = LAT // 2
    upper_days = BLK_ROW // 2
    row_index = jnp.arange(half_rows, dtype=jnp.int32)
    base_days = row_index * (upper_days + 1) // half_rows
    jitter = jax.random.randint(key_days, (half_rows,), -1, 2)
    north_days = jnp.clip(base_days + jitter, 0, upper_days)
    north_days = jnp.where(row_index < ROWS_DEV, 0, north_days)
    all_days = jnp.concatenate([north_days, BLK_ROW - north_days])
    start_block = jax.random.randint(key_start, (LAT,), 0, BLK_ROW)
    column_block = jnp.arange(LON, dtype=jnp.int32) // BCOL
    offset = (column_block[None, :] - start_block[:, None]) % BLK_ROW
    return (offset < all_days[:, None]).astype(jnp.int32)


def block_levels(own_key, extent, cuts, smallest, high):
    def one(axis_at, shards_of):
        draws = jax.random.uniform(jax.random.fold_in(jax.random.fold_in(own_key, 6), axis_at), (shards_of,), jnp.float32, smallest / len(cuts), high / len(cuts))
        return jnp.repeat(jnp.exp(draws), extent[axis_at] // shards_of).reshape((-1,) + (1,) * (len(extent) - axis_at - 1))

    level = one(*cuts[0])
    for cut in cuts[1:]:
        level = level * one(*cut)
    return level


def gaussian(stream_key, extent, spread, bound, pieces=(), kind=jnp.bfloat16):
    drawn = spread * jax.random.normal(stream_key, extent, jnp.float32)
    if pieces:
        drawn = drawn * block_levels(stream_key, extent, pieces, -0.22, 0.18)
    return jnp.clip(drawn, -bound, bound).astype(kind)


def setup_inputs(seed: int = 0) -> dict:
    arg_keys = jax.random.split(jax.random.key(seed), 11)
    column_state = gaussian(arg_keys[0], (LAT, LON, 2 * LEV), 1.0, 6.0, ((0, 256),))
    cosine = jnp.clip(0.2 + 0.8 * jax.random.uniform(arg_keys[1], (LAT, LON), jnp.float32) ** block_levels(arg_keys[1], (LAT, LON), ((0, 256),), -0.2, 0.2), 0.2, 1.0)
    sunlit = draw_sunlit(jax.random.fold_in(arg_keys[10], 71), 0)
    w_in = gaussian(arg_keys[3], (2 * LEV, HID), (2 * LEV) ** -0.5, 0.375)
    w_out = gaussian(arg_keys[4], (HID, LEV), HID ** -0.5, 0.125)
    w_long = gaussian(arg_keys[5], (2 * LEV, LEV), (2 * LEV) ** -0.5, 0.375)
    fourier = gaussian(arg_keys[6], (LAT, M_WIN, 2, 4, LEV), 1.0, 6.0, ((0, 32), (4, 8)))
    quadrature = jnp.clip(jnp.exp(math.log(2.0) - 1.3862944 * jax.random.uniform(arg_keys[7], (LAT,), jnp.float32) ** block_levels(arg_keys[7], (LAT,), ((0, 32),), -0.2, 0.2)), 0.5, 2.0)
    legendre = gaussian(arg_keys[8], (M_WIN, NDEG, LAT), NDEG ** -0.5, 0.25, ((0, 32),))
    damping = jnp.clip(jnp.exp(math.log(1.0) - 2.3025851 * jax.random.uniform(arg_keys[9], (M_WIN, NDEG), jnp.float32) ** block_levels(arg_keys[9], (M_WIN, NDEG), ((0, 32),), -0.2, 0.2)), 0.1, 1.0)
    return dict(column_state=column_state, cosine=cosine, sunlit=sunlit, w_in=w_in, w_out=w_out, w_long=w_long, fourier=fourier, quadrature=quadrature, legendre=legendre, damping=damping)


def fourier_table(count_lon, count_wave):
    longitude = jnp.arange(count_lon, dtype=jnp.int32)
    wavenumber = jnp.arange(count_wave, dtype=jnp.int32)
    phase = longitude[:, None] * wavenumber[None, :] % count_lon
    angle = 2.0 * jnp.pi / count_lon * phase.astype(jnp.float32)
    scale = 1.0 / jnp.sqrt(jnp.float32(count_lon))
    return jnp.concatenate([jnp.cos(angle), -jnp.sin(angle)], axis=1) * scale

def radiation_row(inputs, w_in, w_out, w_long):
    columns, cosine_row, sunlit_row = inputs
    long_wave = jnp.dot(columns, w_long, preferred_element_type=jnp.float32)
    hidden = jax.nn.gelu(jnp.dot(columns, w_in, preferred_element_type=jnp.float32)).astype(jnp.bfloat16)
    short_wave = jnp.dot(hidden, w_out, preferred_element_type=jnp.float32).astype(jnp.bfloat16)
    lighting = sunlit_row.astype(jnp.float32) * cosine_row
    return (long_wave + lighting[:, None] * short_wave.astype(jnp.float32)).astype(jnp.bfloat16)

def reference(column_state, cosine, sunlit, w_in, w_out, w_long, fourier, quadrature, legendre, damping):
    heating = lax.map(lambda inputs: radiation_row(inputs, w_in, w_out, w_long), (column_state, cosine, sunlit))
    table = fourier_table(LON, M_WIN)
    heat_fourier = jnp.einsum('alv,lk->akv', heating.astype(jnp.float32), table, precision=lax.Precision.HIGHEST)
    heat_fourier = heat_fourier.reshape(LAT, 2, M_WIN, LEV).transpose(0, 2, 1, 3)
    warm = fourier.astype(jnp.float32).at[:, :, :, 2, :].add(heat_fourier)
    sent = (quadrature[:, None, None, None, None] * warm).astype(jnp.bfloat16)
    flat = jnp.swapaxes(sent.reshape(LAT, M_WIN, 8 * LEV), 0, 1)

    def one_wave(inputs):
        matrix, values, decay = inputs
        spectral = jnp.dot(matrix, values, preferred_element_type=jnp.float32)
        damped = (spectral * decay[:, None]).astype(jnp.bfloat16)
        return jnp.dot(matrix.T, damped, preferred_element_type=jnp.float32).astype(jnp.bfloat16)
    waves = lax.map(one_wave, (legendre, flat, damping))
    updated = jnp.swapaxes(waves, 0, 1).reshape(LAT, M_WIN, 2, 4, LEV)
    return (heating, updated)
```

```python
import functools

import jax
import jax.numpy as jnp
import ml_dtypes
import numpy as np
from jax import lax
from jax.experimental import pallas as pl
from jax.experimental.pallas import tpu as pltpu
from jax.sharding import PartitionSpec as P

F32 = jnp.float32
BF16 = jnp.bfloat16
LON = 1280
WAVES = 32
CHUNK = 256
HCHUNK = 512
MESH = pl.DeviceIdType.MESH
GELU_A = 0.7978845608028654
GELU_B = 0.7978845608028654 * 0.044715


def nt(a, b):
    return lax.dot_general(a, b, (((1,), (1,)), ((), ())), preferred_element_type=F32)


def nn(a, b):
    return jnp.dot(a, b, preferred_element_type=F32)


def fourier_rows():
    phase = np.arange(LON)[None, :] * np.arange(WAVES)[:, None] % LON
    angle = 2.0 * np.pi / LON * phase
    full = np.stack([np.cos(angle), -np.sin(angle)], axis=1) / np.sqrt(LON)
    high = full.astype(ml_dtypes.bfloat16)
    low = (full - high.astype(np.float64)).astype(ml_dtypes.bfloat16)
    return np.stack([high, low], axis=1).reshape(4 * WAVES, LON)


def gelu2(x):
    x = x.astype(BF16)
    inner = x * (x * x * BF16(GELU_B) + BF16(GELU_A))
    return x + x * jnp.tanh(inner)


def radiation(
    state, cosine, sunlit, w_in, w_out, w_long, table, heating, packed, half_out, light, acc
):
    half_out[...] = (w_out[...].astype(F32) * 0.5).astype(BF16)
    lit = sunlit[...].astype(F32) * cosine[...]
    rows = jnp.concatenate(
        [lit[:, j * 128 : (j + 1) * 128] for j in range(10)] + [jnp.zeros((108, 128), F32)], axis=0
    )
    light[...] = rows.T
    acc[...] = jnp.zeros_like(acc)
    lane = lax.broadcasted_iota(jnp.int32, (128, 128), 1)

    def step(index, carry):
        row = index // 5
        part = index % 5
        here = pl.ds(pl.multiple_of(index * CHUNK, CHUNK), CHUNK)
        x = state[here, :]
        short = jnp.zeros((CHUNK, 128), F32)
        for h in range(0, 2048, HCHUNK):
            hidden = gelu2(nn(x, w_in[:, h : h + HCHUNK]))
            short = short + nn(hidden, half_out[h : h + HCHUNK, :])
        long = nn(x, w_long[...])
        scale = []
        for g in range(2):
            wanted = (part * 2 + g) * 2 + row
            scale.append(jnp.sum(jnp.where(lane == wanted, light[...], 0.0), axis=1, keepdims=True))
        scale = jnp.concatenate(scale, axis=0)
        heat = (long + scale * short.astype(BF16).astype(F32)).astype(BF16)
        heating[here, :] = heat
        cols = pl.ds(pl.multiple_of(part * CHUNK, CHUNK), CHUNK)
        acc[row] += nn(table[:, cols], heat)
        return carry

    lax.fori_loop(0, 10, step, 0)
    first, second = acc[0], acc[1]
    wave_row = lax.broadcasted_iota(jnp.int32, (128, 128), 0)
    both = jnp.where(
        (wave_row % 4) < 2,
        first + pltpu.roll(first, 126, 0),
        second + pltpu.roll(second, 2, 0),
    )
    packed[...] = both.T.astype(BF16).reshape(8, 16, 128)


def spectral_kernel(
    packed, fourier, quad, legendre, damping, updated,
    field_in, send1, recv1, back1, home1, send2, recv2, back2, home2,
    trans, tall, wide, leg_p, leg_t, damp, send_sems, recv_sems,
):
    band = lax.axis_index("band")
    field = lax.axis_index("field")

    barrier = pltpu.get_barrier_semaphore()

    def greet_band(step, carry):
        other = lax.rem(band + step, 32)
        pl.semaphore_signal(barrier, inc=1, device_id=(other, field), device_id_type=MESH)
        return carry

    def greet_field(step, carry):
        other = lax.rem(field + step, 8)
        pl.semaphore_signal(barrier, inc=1, device_id=(band, other), device_id_type=MESH)
        return carry

    lax.fori_loop(1, 8, greet_field, 0)
    lax.fori_loop(1, 32, greet_band, 0)

    def exchange_field(source, target, slot):
        def one(step, carry):
            other = lax.rem(field + step, 8)
            pltpu.make_async_remote_copy(
                src_ref=source.at[other], dst_ref=target.at[field],
                send_sem=send_sems.at[slot], recv_sem=recv_sems.at[slot],
                device_id=(band, other), device_id_type=MESH,
            ).start()
            return carry

        lax.fori_loop(1, 8, one, 0)
        target[field] = source[field]

    def exchange_band(source, target, slot):
        def one(step, carry):
            other = lax.rem(band + step, 32)
            pltpu.make_async_remote_copy(
                src_ref=source.at[other], dst_ref=target.at[band],
                send_sem=send_sems.at[slot], recv_sem=recv_sems.at[slot],
                device_id=(other, field), device_id_type=MESH,
            ).start()
            return carry

        lax.fori_loop(1, 32, one, 0)
        target[band] = source[band]

    def arrived(target, slot, count):
        part = target.at[pl.ds(0, count)]
        pltpu.make_async_copy(part, part, recv_sems.at[slot]).wait()

    def gone(source, slot, count):
        part = source.at[pl.ds(0, count)]
        pltpu.make_async_copy(part, part, send_sems.at[slot]).wait()

    pl.semaphore_wait(barrier, 38)
    exchange_field(packed, field_in, 0)

    eye = (
        lax.broadcasted_iota(jnp.int32, (32, 32), 0) == lax.broadcasted_iota(jnp.int32, (32, 32), 1)
    ).astype(BF16)
    waves = nt(eye, fourier[...])
    lane = lax.broadcasted_iota(jnp.int32, (32, 128), 1)
    for l in range(16):
        trans[pl.ds(l, 32, stride=16), :] = waves[:, l * 128 : (l + 1) * 128] * quad[l]
    send1[...] = trans[...].astype(BF16).reshape(32, 16, 128)
    exchange_band(send1, recv1, 1)

    for row in range(2):
        weight = jnp.zeros((32, 128), F32)
        for z in range(8):
            weight = jnp.where(lane // 16 == z, quad[z * 2 + row], weight)
        for part in range(2):
            k = row * 2 + part
            piece = jnp.zeros((32, 128), F32)
            for z in range(8):
                at = (z * 2 + row) * 128 + part * 64 + 32
                block = waves[:, at // 128 * 128 : at // 128 * 128 + 128]
                moved = pltpu.roll(block, (16 * z - at % 128) % 128, 1)
                piece = jnp.where(lane // 16 == z, moved, piece)
            wide[0, pl.ds(k, 32, stride=4), :] = piece
            wide[1, pl.ds(k, 32, stride=4), :] = weight

    lat = lax.broadcasted_iota(jnp.int32, (512, 512), 0)
    order = lax.broadcasted_iota(jnp.int32, (512, 512), 1)
    shuffle = (lat == (order % 32) * 16 + order // 32).astype(BF16)
    leg_p[...] = nn(legendre[...], shuffle).astype(BF16)
    shuffle_t = (order == (lat % 32) * 16 + lat // 32).astype(BF16)
    leg_t[...] = nt(shuffle_t, legendre[...]).astype(BF16)
    for j in range(5):
        column = jnp.broadcast_to(damping[:, j * 128 : (j + 1) * 128], (128, 128))
        damp[j * 128 : (j + 1) * 128, :] = column.T

    arrived(field_in, 0, 7)
    heat = field_in[...].reshape(128, 128).astype(F32).T
    sent = (wide[1] * (wide[0] + heat)).astype(BF16)
    send2[...] = sent.reshape(32, 4, 128)
    exchange_band(send2, recv2, 2)

    arrived(recv1, 1, 31)
    trans[...] = recv1[...].reshape(512, 128).astype(F32)
    for l in range(16):
        tall[l * 32 : (l + 1) * 32, :] = trans[pl.ds(l, 32, stride=16), :].astype(BF16)
    damped = (nn(leg_p[...], tall[...]) * damp[...]).astype(BF16)
    trans[...] = nn(leg_t[...], damped)
    for b in range(32):
        back1[b] = trans[pl.ds(b, 16, stride=32), :].astype(BF16)
    exchange_band(back1, home1, 3)

    arrived(recv2, 2, 31)
    wide[0] = recv2[...].reshape(128, 128).astype(F32)
    for row in range(2):
        real = wide[0, pl.ds(row * 2, 32, stride=4), :]
        imag = wide[0, pl.ds(row * 2 + 1, 32, stride=4), :]
        for z in range(8):
            l = z * 2 + row
            rolled = jnp.where(
                lane < 16,
                pltpu.roll(real, (128 - 16 * z) % 128, 1),
                pltpu.roll(imag, (144 - 16 * z) % 128, 1),
            )
            tall[l * 32 : (l + 1) * 32, :] = rolled.astype(BF16)
    damped = (nn(leg_p[...], tall[...]) * damp[...]).astype(BF16)
    out = nn(leg_t[...], damped)
    for row in range(2):
        for part in range(2):
            piece = jnp.zeros((32, 128), F32)
            for z in range(8):
                l = z * 2 + row
                moved = pltpu.roll(out[l * 32 : (l + 1) * 32, :], (16 * z - 16 * part) % 128, 1)
                piece = jnp.where(lane // 16 == z, moved, piece)
            wide[0, pl.ds(row * 2 + part, 32, stride=4), :] = piece
    back2[...] = wide[0].astype(BF16).reshape(32, 4, 128)
    exchange_band(back2, home2, 4)

    arrived(home1, 3, 31)
    trans[...] = home1[...].reshape(512, 128).astype(F32)
    for l in range(16):
        piece = trans[pl.ds(l, 32, stride=16), :].T
        updated[l // 2, l % 2] = piece.astype(BF16).reshape(2, 4, 16, 32)
    arrived(home2, 4, 31)
    wide[0] = home2[...].reshape(128, 128).astype(F32)
    for k in range(4):
        piece = wide[0, pl.ds(k, 32, stride=4), :].T
        updated[:, k // 2, k % 2, 2] = piece.astype(BF16).reshape(8, 16, 32)

    gone(packed, 0, 7)
    gone(send1, 1, 31)
    gone(send2, 2, 31)
    gone(back1, 3, 31)
    gone(back2, 4, 31)


def local(
    column_state, cosine, sunlit, w_in, w_out, w_long, fourier, quadrature, legendre, damping
):
    vmem = pl.BlockSpec(memory_space=pltpu.VMEM)
    smem = pl.BlockSpec(memory_space=pltpu.SMEM)
    table = jnp.asarray(fourier_rows())
    heating, packed = pl.pallas_call(
        radiation,
        out_shape=(
            jax.ShapeDtypeStruct((2560, 128), BF16),
            jax.ShapeDtypeStruct((8, 16, 128), BF16),
        ),
        in_specs=[vmem] * 7,
        out_specs=(vmem, vmem),
        scratch_shapes=[
            pltpu.VMEM((2048, 128), BF16),
            pltpu.VMEM((128, 128), F32),
            pltpu.VMEM((2, 128, 128), F32),
        ],
        compiler_params=pltpu.CompilerParams(vmem_limit_bytes=40 * 2**20),
        name="radiation",
    )(column_state.reshape(2560, 256), cosine, sunlit, w_in, w_out, w_long, table)

    flat = fourier.transpose(0, 2, 3, 4, 1).reshape(2048, 32)
    whole = pltpu.VMEM((32, 16, 128), BF16)
    small = pltpu.VMEM((32, 4, 128), BF16)
    updated = pl.pallas_call(
        spectral_kernel,
        out_shape=jax.ShapeDtypeStruct((8, 2, 2, 4, 16, 32), BF16),
        in_specs=[vmem, vmem, smem, vmem, vmem],
        out_specs=vmem,
        scratch_shapes=[
            pltpu.VMEM((8, 16, 128), BF16),
            whole, whole, whole, whole,
            small, small, small, small,
            pltpu.VMEM((512, 128), F32),
            pltpu.VMEM((512, 128), BF16),
            pltpu.VMEM((2, 128, 128), F32),
            pltpu.VMEM((640, 512), BF16),
            pltpu.VMEM((512, 640), BF16),
            pltpu.VMEM((640, 128), F32),
            pltpu.SemaphoreType.DMA((5,)),
            pltpu.SemaphoreType.DMA((5,)),
        ],
        compiler_params=pltpu.CompilerParams(
            collective_id=0, has_side_effects=True, vmem_limit_bytes=32 * 2**20
        ),
        name="spectral",
    )(packed, flat, quadrature, legendre.reshape(640, 512), damping)
    updated = updated.reshape(16, 2, 4, 16, 32).transpose(0, 4, 1, 2, 3)
    return heating.reshape(2, 1280, 128), updated


def solution(mesh):
    in_specs = (
        P(("band", "field"), None, None),
        P(("band", "field"), None),
        P(("band", "field"), None),
        P(),
        P(),
        P(),
        P("band", None, None, None, "field"),
        P("band"),
        P("band", None, None),
        P("band", None),
    )
    out_specs = (P(("band", "field"), None, None), P("band", None, None, None, "field"))
    return jax.shard_map(local, mesh=mesh, in_specs=in_specs, out_specs=out_specs, check_vma=False)
```

```python
import functools

import jax
import jax.numpy as jnp
import ml_dtypes
import numpy as np
from jax import lax
from jax.experimental import pallas as pl
from jax.experimental.pallas import tpu as pltpu
from jax.sharding import PartitionSpec as P

F32 = jnp.float32
BF16 = jnp.bfloat16
LON = 1280
WAVES = 32
HCHUNK = 512
ALL_VMEM = 64 * 2**20 - 65536
FINISH_VMEM = 2**20
MESH = pl.DeviceIdType.MESH
GELU_A = 0.7978845608028654
GELU_B = 0.7978845608028654 * 0.044715


def nt(a, b):
    return lax.dot_general(a, b, (((1,), (1,)), ((), ())), preferred_element_type=F32)


def nn(a, b):
    return jnp.dot(a, b, preferred_element_type=F32)


def fourier_rows():
    phase = np.arange(LON)[None, :] * np.arange(WAVES)[:, None] % LON
    angle = 2.0 * np.pi / LON * phase
    full = np.stack([np.cos(angle), -np.sin(angle)], axis=1) / np.sqrt(LON)
    high = full.astype(ml_dtypes.bfloat16)
    low = (full - high.astype(np.float64)).astype(ml_dtypes.bfloat16)
    return np.stack([high, low], axis=1).reshape(4 * WAVES, LON).T.copy()


def gelu2(x):
    x = x.astype(BF16)
    inner = x * (x * x * BF16(GELU_B) + BF16(GELU_A))
    return x + x * jnp.tanh(inner)


def eye(n):
    row = lax.broadcasted_iota(jnp.int32, (n, n), 0)
    return (row == lax.broadcasted_iota(jnp.int32, (n, n), 1)).astype(BF16)


def kernel(
    state_hbm, cosine_hbm, sunlit_hbm, w_in_hbm, w_out_hbm, w_long_hbm, table_hbm,
    fourier_hbm, quad_hbm, legendre_hbm, damping_hbm,
    heating, updated,
    state, cosine, sunlit, w_in, w_out, w_long, table, fourier, quad, legendre, damping,
    in_t, out_t, long_t, heat_t, packed,
    field_in, send1, recv1, back1, home1, send2, recv2, back2, home2,
    trans, tall, wide, leg_p, leg_t, damp, load_sems, send_sems, recv_sems,
):
    loads = [
        pltpu.make_async_copy(source, target, load_sems.at[i])
        for i, (source, target) in enumerate(
            (
                (w_in_hbm, w_in),
                (w_out_hbm, w_out),
                (w_long_hbm, w_long),
                (state_hbm, state),
                (cosine_hbm, cosine),
                (sunlit_hbm, sunlit),
                (table_hbm, table),
                (fourier_hbm, fourier),
                (quad_hbm, quad),
                (legendre_hbm, legendre),
                (damping_hbm, damping),
            )
        )
    ]
    for load in loads:
        load.start()

    band = lax.axis_index("band")
    field = lax.axis_index("field")

    barrier = pltpu.get_barrier_semaphore()

    def greet_band(step, carry):
        other = lax.rem(band + step, 32)
        pl.semaphore_signal(barrier, inc=1, device_id=(other, field), device_id_type=MESH)
        return carry

    def greet_field(step, carry):
        other = lax.rem(field + step, 8)
        pl.semaphore_signal(barrier, inc=1, device_id=(band, other), device_id_type=MESH)
        return carry

    lax.fori_loop(1, 8, greet_field, 0)
    lax.fori_loop(1, 32, greet_band, 0)

    def exchange_field(source, target, slot):
        def one(step, carry):
            other = lax.rem(field + step, 8)
            pltpu.make_async_remote_copy(
                src_ref=source.at[other], dst_ref=target.at[field],
                send_sem=send_sems.at[slot], recv_sem=recv_sems.at[slot],
                device_id=(band, other), device_id_type=MESH,
            ).start()
            return carry

        lax.fori_loop(1, 8, one, 0)
        target[field] = source[field]

    def exchange_band(source, target, slot):
        def one(step, carry):
            other = lax.rem(band + step, 32)
            pltpu.make_async_remote_copy(
                src_ref=source.at[other], dst_ref=target.at[band],
                send_sem=send_sems.at[slot], recv_sem=recv_sems.at[slot],
                device_id=(other, field), device_id_type=MESH,
            ).start()
            return carry

        lax.fori_loop(1, 32, one, 0)
        target[band] = source[band]

    def arrived(target, slot, count):
        part = target.at[pl.ds(0, count)]
        pltpu.make_async_copy(part, part, recv_sems.at[slot]).wait()

    def gone(source, slot, count):
        part = source.at[pl.ds(0, count)]
        pltpu.make_async_copy(part, part, send_sems.at[slot]).wait()

    loads[0].wait()
    for h in range(0, 2048, 256):
        in_t[h : h + 256, :] = nt(eye(256), w_in[:, h : h + 256]).astype(BF16)
    loads[1].wait()
    loads[2].wait()
    out_t[...] = (nt(eye(128), w_out[...]) * 0.5).astype(BF16)
    long_t[...] = nt(eye(128), w_long[...]).astype(BF16)
    for load in loads[3:6]:
        load.wait()
    x = state[...]
    short = jnp.zeros((128, 2560), F32)
    ahead = nt(in_t[:HCHUNK, :], x)
    for h in range(0, 2048, HCHUNK):
        raw = ahead
        if h + HCHUNK < 2048:
            ahead = nt(in_t[h + HCHUNK : h + 2 * HCHUNK, :], x)
        short = short + nn(out_t[:, h : h + HCHUNK], gelu2(raw))
    long = nt(long_t[...], x)
    light = sunlit[...].astype(F32) * cosine[...]
    light = jnp.concatenate([light[0:1, :], light[1:2, :]], axis=1)
    heat_t[...] = (long + light * short.astype(BF16).astype(F32)).astype(BF16)

    loads[6].wait()
    first = nn(heat_t[:, :LON], table[...])
    second = nn(heat_t[:, LON:], table[...])
    wave_lane = lax.broadcasted_iota(jnp.int32, (128, 128), 1)
    both = jnp.where(
        (wave_lane % 4) < 2,
        first + pltpu.roll(first, 126, 1),
        second + pltpu.roll(second, 2, 1),
    )
    packed[...] = both.astype(BF16).reshape(8, 16, 128)

    pl.semaphore_wait(barrier, 38)
    exchange_field(packed, field_in, 0)
    for load in loads[7:]:
        load.wait()

    waves = nt(eye(32), fourier[...])
    lane = lax.broadcasted_iota(jnp.int32, (32, 128), 1)
    for l in range(16):
        trans[pl.ds(l, 32, stride=16), :] = waves[:, l * 128 : (l + 1) * 128] * quad[l]
    send1[...] = trans[...].astype(BF16).reshape(32, 16, 128)
    exchange_band(send1, recv1, 1)

    for row in range(2):
        weight = jnp.zeros((32, 128), F32)
        for z in range(8):
            weight = jnp.where(lane // 16 == z, quad[z * 2 + row], weight)
        for part in range(2):
            k = row * 2 + part
            piece = jnp.zeros((32, 128), F32)
            for z in range(8):
                at = (z * 2 + row) * 128 + part * 64 + 32
                block = waves[:, at // 128 * 128 : at // 128 * 128 + 128]
                moved = pltpu.roll(block, (16 * z - at % 128) % 128, 1)
                piece = jnp.where(lane // 16 == z, moved, piece)
            wide[0, pl.ds(k, 32, stride=4), :] = piece
            wide[1, pl.ds(k, 32, stride=4), :] = weight

    lat = lax.broadcasted_iota(jnp.int32, (512, 512), 0)
    order = lax.broadcasted_iota(jnp.int32, (512, 512), 1)
    shuffle = (lat == (order % 32) * 16 + order // 32).astype(BF16)
    leg_p[...] = nn(legendre[...], shuffle).astype(BF16)
    shuffle_t = (order == (lat % 32) * 16 + lat // 32).astype(BF16)
    leg_t[...] = nt(shuffle_t, legendre[...]).astype(BF16)
    for j in range(5):
        column = jnp.broadcast_to(damping[:, j * 128 : (j + 1) * 128], (128, 128))
        damp[j * 128 : (j + 1) * 128, :] = column.T

    for j in range(0, 2560, 256):
        heating[j : j + 256, :] = heat_t[:, j : j + 256].astype(F32).T.astype(BF16)

    arrived(field_in, 0, 7)
    heat = field_in[...].reshape(128, 128).astype(F32).T
    sent = (wide[1] * (wide[0] + heat)).astype(BF16)
    send2[...] = sent.reshape(32, 4, 128)
    exchange_band(send2, recv2, 2)

    arrived(recv1, 1, 31)
    trans[...] = recv1[...].reshape(512, 128).astype(F32)
    for l in range(16):
        tall[l * 32 : (l + 1) * 32, :] = trans[pl.ds(l, 32, stride=16), :].astype(BF16)
    damped = (nn(leg_p[...], tall[...]) * damp[...]).astype(BF16)
    trans[...] = nn(leg_t[...], damped)
    for b in range(32):
        back1[b] = trans[pl.ds(b, 16, stride=32), :].astype(BF16)
    exchange_band(back1, home1, 3)

    arrived(recv2, 2, 31)
    wide[0] = recv2[...].reshape(128, 128).astype(F32)
    for row in range(2):
        real = wide[0, pl.ds(row * 2, 32, stride=4), :]
        imag = wide[0, pl.ds(row * 2 + 1, 32, stride=4), :]
        for z in range(8):
            l = z * 2 + row
            rolled = jnp.where(
                lane < 16,
                pltpu.roll(real, (128 - 16 * z) % 128, 1),
                pltpu.roll(imag, (144 - 16 * z) % 128, 1),
            )
            tall[l * 32 : (l + 1) * 32, :] = rolled.astype(BF16)
    damped = (nn(leg_p[...], tall[...]) * damp[...]).astype(BF16)
    out = nn(leg_t[...], damped)
    for row in range(2):
        for part in range(2):
            piece = jnp.zeros((32, 128), F32)
            for z in range(8):
                l = z * 2 + row
                moved = pltpu.roll(out[l * 32 : (l + 1) * 32, :], (16 * z - 16 * part) % 128, 1)
                piece = jnp.where(lane // 16 == z, moved, piece)
            wide[0, pl.ds(row * 2 + part, 32, stride=4), :] = piece
    back2[...] = wide[0].astype(BF16).reshape(32, 4, 128)
    exchange_band(back2, home2, 4)

    arrived(home1, 3, 31)
    trans[...] = home1[...].reshape(512, 128).astype(F32)
    for l in range(16):
        piece = trans[pl.ds(l, 32, stride=16), :].T
        updated[l // 2, l % 2] = piece.astype(BF16).reshape(2, 4, 16, 32)
    arrived(home2, 4, 31)
    wide[0] = home2[...].reshape(128, 128).astype(F32)
    for k in range(4):
        piece = wide[0, pl.ds(k, 32, stride=4), :].T
        updated[:, k // 2, k % 2, 2] = piece.astype(BF16).reshape(8, 16, 32)

    gone(packed, 0, 7)
    gone(send1, 1, 31)
    gone(send2, 2, 31)
    gone(back1, 3, 31)
    gone(back2, 4, 31)


def finish(heating, updated, heating_out, updated_out, sems):
    copies = []
    for i in range(4):
        part = pl.ds(i * 640, 640)
        copies.append(pltpu.make_async_copy(heating.at[part], heating_out.at[part], sems.at[i]))
    for i in range(2):
        part = pl.ds(i * 4, 4)
        copies.append(pltpu.make_async_copy(updated.at[part], updated_out.at[part], sems.at[4 + i]))
    for copy in copies:
        copy.start()
    for copy in copies:
        copy.wait()


def local(
    column_state, cosine, sunlit, w_in, w_out, w_long, fourier, quadrature, legendre, damping
):
    hbm = pl.BlockSpec(memory_space=pltpu.HBM)
    vmem = pl.BlockSpec(memory_space=pltpu.VMEM)
    anywhere = pl.BlockSpec(memory_space=pl.ANY)
    operands = (
        column_state.reshape(2560, 256),
        cosine,
        sunlit,
        w_in,
        w_out,
        w_long,
        jnp.asarray(fourier_rows()),
        fourier.transpose(0, 2, 3, 4, 1).reshape(2048, 32),
        quadrature,
        legendre.reshape(640, 512),
        damping,
    )
    held = [pltpu.VMEM(x.shape, x.dtype) for x in operands]
    held[8] = pltpu.SMEM((16,), F32)
    whole = pltpu.VMEM((32, 16, 128), BF16)
    small = pltpu.VMEM((32, 4, 128), BF16)
    heating, updated = pl.pallas_call(
        kernel,
        out_shape=(
            pltpu.VMEM((2560, 128), BF16),
            pltpu.VMEM((8, 2, 2, 4, 16, 32), BF16),
        ),
        in_specs=[hbm] * len(operands),
        out_specs=(vmem, vmem),
        scratch_shapes=held
        + [
            pltpu.VMEM((2048, 256), BF16),
            pltpu.VMEM((128, 2048), BF16),
            pltpu.VMEM((128, 256), BF16),
            pltpu.VMEM((128, 2560), BF16),
            pltpu.VMEM((8, 16, 128), BF16),
            pltpu.VMEM((8, 16, 128), BF16),
            whole, whole, whole, whole,
            small, small, small, small,
            pltpu.VMEM((512, 128), F32),
            pltpu.VMEM((512, 128), BF16),
            pltpu.VMEM((2, 128, 128), F32),
            pltpu.VMEM((640, 512), BF16),
            pltpu.VMEM((512, 640), BF16),
            pltpu.VMEM((640, 128), F32),
            pltpu.SemaphoreType.DMA((len(operands),)),
            pltpu.SemaphoreType.DMA((5,)),
            pltpu.SemaphoreType.DMA((5,)),
        ],
        compiler_params=pltpu.CompilerParams(
            collective_id=0, has_side_effects=True, vmem_limit_bytes=48 * 2**20
        ),
        name="step",
    )(*[pltpu.with_memory_space_constraint(x, pltpu.HBM) for x in operands])
    heating, updated = pl.pallas_call(
        finish,
        out_shape=(
            jax.ShapeDtypeStruct((2560, 128), BF16),
            jax.ShapeDtypeStruct((8, 2, 2, 4, 16, 32), BF16),
        ),
        in_specs=[anywhere] * 2,
        out_specs=(anywhere, anywhere),
        scratch_shapes=[pltpu.SemaphoreType.DMA((6,))],
        compiler_params=pltpu.CompilerParams(vmem_limit_bytes=FINISH_VMEM),
        name="finish",
    )(heating, updated)
    updated = updated.reshape(16, 2, 4, 16, 32).transpose(0, 4, 1, 2, 3)
    return heating.reshape(2, 1280, 128), updated


def solution(mesh):
    in_specs = (
        P(("band", "field"), None, None),
        P(("band", "field"), None),
        P(("band", "field"), None),
        P(),
        P(),
        P(),
        P("band", None, None, None, "field"),
        P("band"),
        P("band", None, None),
        P("band", None),
    )
    out_specs = (P(("band", "field"), None, None), P("band", None, None, None, "field"))
    return jax.shard_map(local, mesh=mesh, in_specs=in_specs, out_specs=out_specs, check_vma=False)
```

```python
import jax
import jax.numpy as jnp
import ml_dtypes
import numpy as np
from jax import lax
from jax.experimental import pallas as pl
from jax.experimental.pallas import tpu as pltpu
from jax.sharding import PartitionSpec as P

F32 = jnp.float32
BF16 = jnp.bfloat16
LON = 1280
WAVES = 32
HCHUNK = 512
CHUNK = 256
ALL_VMEM = 64 * 2**20 - 65536
FINISH_VMEM = 2**20
MESH = pl.DeviceIdType.MESH
GELU_A = 0.7978845608028654
GELU_B = 0.7978845608028654 * 0.044715


def nt(a, b):
    return lax.dot_general(a, b, (((1,), (1,)), ((), ())), preferred_element_type=F32)


def nn(a, b):
    return jnp.dot(a, b, preferred_element_type=F32)


def place(z):
    return (z % 4) * 2 + z // 4


def fourier_rows():
    phase = np.arange(LON)[None, :] * np.arange(WAVES)[:, None] % LON
    angle = 2.0 * np.pi / LON * phase
    full = np.stack([np.cos(angle), -np.sin(angle)]) / np.sqrt(LON)
    high = full.astype(ml_dtypes.bfloat16)
    low = (full - high.astype(np.float64)).astype(ml_dtypes.bfloat16)
    return np.stack([high, low]).reshape(4 * WAVES, 10, 128).swapaxes(0, 1).copy()


def gelu2(x):
    x = x.astype(BF16)
    inner = x * (x * x * BF16(GELU_B) + BF16(GELU_A))
    return x + x * jnp.tanh(inner)


def eye(n):
    row = lax.broadcasted_iota(jnp.int32, (n, n), 0)
    return (row == lax.broadcasted_iota(jnp.int32, (n, n), 1)).astype(BF16)


def kernel(
    state_hbm, cosine_hbm, sunlit_hbm, w_in_hbm, w_out_hbm, w_long_hbm, table_hbm,
    fourier_hbm, quad_hbm, legendre_hbm, damping_hbm,
    heating, updated,
    state, cosine, sunlit, w_in, w_out, w_long, table, fourier, quad, legendre, damping,
    in_t, out_t, hidden, long_wave, heat_t, sent_all, got_all,
    send1, recv1, back1, home1, back2, home2,
    trans, tall, wide, leg_p, leg_t, damp, load_sems, send_sems, recv_sems,
):
    loads = [
        pltpu.make_async_copy(source, target, load_sems.at[i])
        for i, (source, target) in enumerate(
            (
                (w_out_hbm, w_out),
                (w_long_hbm, w_long),
                (w_in_hbm, w_in),
                (state_hbm, state),
                (cosine_hbm, cosine),
                (sunlit_hbm, sunlit),
                (table_hbm, table),
                (quad_hbm, quad),
                (fourier_hbm, fourier),
                (legendre_hbm, legendre),
                (damping_hbm, damping),
            )
        )
    ]
    for load in loads[:6]:
        load.start()

    band = lax.axis_index("band")
    field = lax.axis_index("field")
    x, y, core = band // 8, lax.rem(band // 2, 4), lax.rem(band, 2)

    bands = [
        lax.rem(x + i, 4) * 8 + lax.rem(y + j, 4) * 2 + lax.rem(core + k, 2)
        for i, j in ((2, 2), (2, 1), (2, 3), (1, 2), (3, 2), (2, 0), (0, 2), (1, 1), (1, 3), (3, 1))
        + ((3, 3), (1, 0), (3, 0), (0, 1), (0, 3), (0, 0))
        for k in (1, 0)
    ]

    def ring(start, stop, act):
        def one_field(t, carry):
            near = (t + 1) // 2
            other = lax.rem(field + 12 + near * (1 - 2 * lax.rem(t, 2)), 8)
            for other_band in bands:
                act(other_band, other)
            return carry

        lax.fori_loop(start, stop, one_field, 0)

    def plane(act):
        for other_band in bands[:-1]:
            act(other_band, field)

    barrier = pltpu.get_barrier_semaphore()

    def greet(other_band, other_field):
        pl.semaphore_signal(
            barrier, inc=1, device_id=(other_band, other_field), device_id_type=MESH
        )

    ring(0, 7, greet)
    plane(greet)

    def exchange_band(source, target, slot):
        def one(other_band, other_field):
            pltpu.make_async_remote_copy(
                src_ref=source.at[other_band], dst_ref=target.at[band],
                send_sem=send_sems.at[slot], recv_sem=recv_sems.at[slot],
                device_id=(other_band, other_field), device_id_type=MESH,
            ).start()

        plane(one)
        target[band] = source[band]

    def arrived(target, slot, count):
        part = target.at[pl.ds(0, count)]
        pltpu.make_async_copy(part, part, recv_sems.at[slot]).wait()

    def gone(source, slot, count):
        part = source.at[pl.ds(0, count)]
        pltpu.make_async_copy(part, part, send_sems.at[slot]).wait()

    loads[0].wait()
    loads[1].wait()
    out_t[...] = (nt(eye(128), w_out[...]) * 0.5).astype(BF16)
    in_t[2048:, :] = nt(eye(128), w_long[...]).astype(BF16)
    loads[2].wait()
    for h in range(0, 2048, 256):
        in_t[h : h + 256, :] = nt(eye(256), w_in[:, h : h + 256]).astype(BF16)
    loads[3].wait()
    for load in loads[6:]:
        load.start()
    for h in range(0, 2048, HCHUNK):
        hidden[h : h + HCHUNK, :] = gelu2(nt(in_t[h : h + HCHUNK, :], state[...]))
    long_wave[...] = nt(in_t[2048:, :], state[...])
    loads[4].wait()
    loads[5].wait()
    light = sunlit[...].astype(F32) * cosine[...]
    light = jnp.concatenate([light[0:1, :], light[1:2, :]], axis=1)
    for c in range(0, 2560, CHUNK):
        here = slice(c, c + CHUNK)
        short = nn(out_t[...], hidden[:, here]).astype(BF16).astype(F32)
        heat_t[:, here] = (long_wave[:, here] + light[:, here] * short).astype(BF16)

    loads[6].wait()
    loads[7].wait()
    lane = lax.broadcasted_iota(jnp.int32, (32, 128), 1)
    pieces = []
    rows = jnp.concatenate([table[i] for i in range(10)], axis=1)
    for row in range(2):
        both = nt(rows, heat_t[:, row * LON : (row + 1) * LON])
        weight = quad[field * 2 + row]
        pieces += [(both[i : i + 32, :] + both[i + 64 : i + 96, :]) * weight for i in (0, 32)]
    for z in range(8):
        block = jnp.zeros((32, 128), F32)
        for k in range(4):
            moved = pltpu.roll(pieces[k], (16 * (k - z)) % 128, 1)
            block = jnp.where(lane // 16 == k, moved, block)
        sent_all[z * 32 : (z + 1) * 32, :] = block

    mine = pl.ds(band * 8 + lax.rem(field, 4) * 2 + field // 4, 1)

    def send_heat(other_band, other_field):
        pltpu.make_async_remote_copy(
            src_ref=sent_all.at[pl.ds(other_field * 32 + other_band, 1)], dst_ref=got_all.at[mine],
            send_sem=send_sems.at[0], recv_sem=recv_sems.at[0],
            device_id=(other_band, other_field), device_id_type=MESH,
        ).start()

    pl.semaphore_wait(barrier, 255)
    ring(0, 7, send_heat)
    plane(send_heat)
    got_all[mine, :] = sent_all[pl.ds(field * 32 + band, 1), :]

    loads[8].wait()
    waves = nt(eye(32), fourier[...])
    for l in range(16):
        j = place(l // 2) * 2 + l % 2
        trans[pl.ds(j, 32, stride=16), :] = waves[:, l * 128 : (l + 1) * 128] * quad[l]
    send1[...] = trans[...].astype(BF16).reshape(32, 16, 128)
    exchange_band(send1, recv1, 1)

    loads[9].wait()
    loads[10].wait()

    def latitude(order):
        spot = order % 8
        return order % 256 // 8 * 16 + (spot % 2 * 4 + spot // 2) * 2 + order // 256

    down = lax.broadcasted_iota(jnp.int32, (512, 512), 0)
    across = lax.broadcasted_iota(jnp.int32, (512, 512), 1)
    leg_p[...] = nn(legendre[...], (down == latitude(across)).astype(BF16)).astype(BF16)
    leg_t[...] = nt((across == latitude(down)).astype(BF16), legendre[...]).astype(BF16)
    for j in range(5):
        column = jnp.broadcast_to(damping[:, j * 128 : (j + 1) * 128], (128, 128))
        damp[j * 128 : (j + 1) * 128, :] = column.T
    for j in range(0, 2560, 256):
        heating[j : j + 256, :] = heat_t[:, j : j + 256].astype(F32).T.astype(BF16)

    arrived(recv1, 1, 31)
    trans[...] = recv1[...].reshape(512, 128).astype(F32)
    lane = lax.broadcasted_iota(jnp.int32, (256, 128), 1)
    cool = jnp.zeros((256, 128), F32)
    for row in range(2):
        half = trans[pl.ds(row, 256, stride=2), :]
        tall[row * 256 : (row + 1) * 256, :] = half.astype(BF16)
        for part in range(2):
            k = row * 2 + part
            moved = pltpu.roll(half, (16 * k - 64 * part - 32) % 128, 1)
            cool = jnp.where(lane // 16 == k, moved, cool)
    wide[...] = cool
    damped = (nn(leg_p[...], tall[...]) * damp[...]).astype(BF16)
    out = nn(leg_t[...], damped)
    for row in range(2):
        trans[pl.ds(row, 256, stride=2), :] = out[row * 256 : (row + 1) * 256, :]
    back1[...] = trans[...].astype(BF16).reshape(32, 16, 128)
    exchange_band(back1, home1, 2)

    arrived(got_all, 0, 255)
    warm = wide[...] + got_all[...]
    tall[:256, :] = warm.astype(BF16)
    tall[256:, :] = pltpu.roll(warm, 96, 1).astype(BF16)
    damped = (nn(leg_p[...], tall[...]) * damp[...]).astype(BF16)
    out = nn(leg_t[...], damped)
    wide[...] = jnp.where(lane < 32, out[:256, :], pltpu.roll(out[256:, :], 32, 1))
    pair = jnp.where(
        lane[:128, :] < 64,
        wide[pl.ds(0, 128, stride=2), :],
        pltpu.roll(wide[pl.ds(1, 128, stride=2), :], 64, 1),
    )
    back2[...] = pair.astype(BF16).reshape(32, 4, 128)
    exchange_band(back2, home2, 3)

    arrived(home1, 2, 31)
    trans[...] = home1[...].reshape(512, 128).astype(F32)
    for l in range(16):
        j = place(l // 2) * 2 + l % 2
        piece = trans[pl.ds(j, 32, stride=16), :].T
        updated[l // 2, l % 2] = piece.astype(BF16).reshape(2, 4, 16, 32)
    arrived(home2, 3, 31)
    wide[:128, :] = home2[...].reshape(128, 128).astype(F32)
    for low in range(4):
        piece = wide[pl.ds(low, 32, stride=4), :].T.astype(BF16).reshape(2, 2, 2, 16, 32)
        for high in range(2):
            updated[high * 4 + low, :, :, 2] = piece[high]

    gone(got_all, 0, 255)
    gone(send1, 1, 31)
    gone(back1, 2, 31)
    gone(back2, 3, 31)


def finish(heating, updated, heating_out, updated_out, sems):
    copies = []
    for i in range(4):
        part = pl.ds(i * 640, 640)
        copies.append(pltpu.make_async_copy(heating.at[part], heating_out.at[part], sems.at[i]))
    for i in range(2):
        part = pl.ds(i * 4, 4)
        copies.append(pltpu.make_async_copy(updated.at[part], updated_out.at[part], sems.at[4 + i]))
    for copy in copies:
        copy.start()
    for copy in copies:
        copy.wait()


def local(
    column_state, cosine, sunlit, w_in, w_out, w_long, fourier, quadrature, legendre, damping
):
    hbm = pl.BlockSpec(memory_space=pltpu.HBM)
    vmem = pl.BlockSpec(memory_space=pltpu.VMEM)
    anywhere = pl.BlockSpec(memory_space=pl.ANY)
    operands = (
        column_state.reshape(2560, 256),
        cosine,
        sunlit,
        w_in,
        w_out,
        w_long,
        jnp.asarray(fourier_rows()),
        fourier.transpose(0, 2, 3, 4, 1).reshape(2048, 32),
        quadrature,
        legendre.reshape(640, 512),
        damping,
    )
    held = [pltpu.VMEM(x.shape, x.dtype) for x in operands]
    held[8] = pltpu.SMEM((16,), F32)
    whole = pltpu.VMEM((32, 16, 128), BF16)
    small = pltpu.VMEM((32, 4, 128), BF16)
    heating, updated = pl.pallas_call(
        kernel,
        out_shape=(
            pltpu.VMEM((2560, 128), BF16),
            pltpu.VMEM((8, 2, 2, 4, 16, 32), BF16),
        ),
        in_specs=[hbm] * len(operands),
        out_specs=(vmem, vmem),
        scratch_shapes=held
        + [
            pltpu.VMEM((2176, 256), BF16),
            pltpu.VMEM((128, 2048), BF16),
            pltpu.VMEM((2048, 2560), BF16),
            pltpu.VMEM((128, 2560), F32),
            pltpu.VMEM((128, 2560), BF16),
            pltpu.VMEM((256, 128), F32),
            pltpu.VMEM((256, 128), F32),
            whole, whole, whole, whole,
            small, small,
            pltpu.VMEM((512, 128), F32),
            pltpu.VMEM((512, 128), BF16),
            pltpu.VMEM((256, 128), F32),
            pltpu.VMEM((640, 512), BF16),
            pltpu.VMEM((512, 640), BF16),
            pltpu.VMEM((640, 128), F32),
            pltpu.SemaphoreType.DMA((len(operands),)),
            pltpu.SemaphoreType.DMA((4,)),
            pltpu.SemaphoreType.DMA((4,)),
        ],
        compiler_params=pltpu.CompilerParams(
            collective_id=0, has_side_effects=True, vmem_limit_bytes=48 * 2**20
        ),
        name="step",
    )(*[pltpu.with_memory_space_constraint(x, pltpu.HBM) for x in operands])
    heating, updated = pl.pallas_call(
        finish,
        out_shape=(
            jax.ShapeDtypeStruct((2560, 128), BF16),
            jax.ShapeDtypeStruct((8, 2, 2, 4, 16, 32), BF16),
        ),
        in_specs=[anywhere] * 2,
        out_specs=(anywhere, anywhere),
        scratch_shapes=[pltpu.SemaphoreType.DMA((6,))],
        compiler_params=pltpu.CompilerParams(vmem_limit_bytes=FINISH_VMEM),
        name="finish",
    )(heating, updated)
    updated = updated.reshape(16, 2, 4, 16, 32).transpose(0, 4, 1, 2, 3)
    return heating.reshape(2, 1280, 128), updated


def solution(mesh):
    in_specs = (
        P(("band", "field"), None, None),
        P(("band", "field"), None),
        P(("band", "field"), None),
        P(),
        P(),
        P(),
        P("band", None, None, None, "field"),
        P("band"),
        P("band", None, None),
        P("band", None),
    )
    out_specs = (P(("band", "field"), None, None), P("band", None, None, None, "field"))
    return jax.shard_map(local, mesh=mesh, in_specs=in_specs, out_specs=out_specs, check_vma=False)
```

```python
import jax
import jax.numpy as jnp
import ml_dtypes
import numpy as np
from jax import lax
from jax.experimental import pallas as pl
from jax.experimental.pallas import tpu as pltpu
from jax.sharding import PartitionSpec as P

F32 = jnp.float32
BF16 = jnp.bfloat16
LON = 1280
WAVES = 32
HCHUNK = 512
CHUNK = 256
ALL_VMEM = 64 * 2**20 - 65536
FINISH_VMEM = 2**20
MESH = pl.DeviceIdType.MESH
GELU_A = 0.7978845608028654
GELU_B = 0.7978845608028654 * 0.044715


def nt(a, b):
    return lax.dot_general(a, b, (((1,), (1,)), ((), ())), preferred_element_type=F32)


def nn(a, b):
    return jnp.dot(a, b, preferred_element_type=F32)


def place(z):
    return (z % 4) * 2 + z // 4


def fourier_rows():
    phase = np.arange(LON)[None, :] * np.arange(WAVES)[:, None] % LON
    angle = 2.0 * np.pi / LON * phase
    full = np.stack([np.cos(angle), -np.sin(angle)]) / np.sqrt(LON)
    high = full.astype(ml_dtypes.bfloat16)
    low = (full - high.astype(np.float64)).astype(ml_dtypes.bfloat16)
    return np.stack([high, low]).reshape(4 * WAVES, 10, 128).swapaxes(0, 1).copy()


def gelu2(x):
    x = x.astype(BF16)
    inner = x * (x * x * BF16(GELU_B) + BF16(GELU_A))
    return x + x * jnp.tanh(inner)


def eye(n):
    row = lax.broadcasted_iota(jnp.int32, (n, n), 0)
    return (row == lax.broadcasted_iota(jnp.int32, (n, n), 1)).astype(BF16)


def kernel(
    state_hbm, cosine_hbm, sunlit_hbm, w_in_hbm, w_out_hbm, w_long_hbm, table_hbm,
    fourier_hbm, quad_hbm, legendre_hbm, damping_hbm,
    heating, updated,
    state, cosine, sunlit, w_in, w_out, w_long, table, fourier, quad, legendre, damping,
    in_t, out_t, hidden, long_wave, heat_t, sent_all, got_all,
    send1, recv1, back1, home1, back2, home2,
    trans, tall, wide, leg_p, leg_t, damp, load_sems, send_sems, recv_sems,
):
    loads = [
        pltpu.make_async_copy(source, target, load_sems.at[i])
        for i, (source, target) in enumerate(
            (
                (w_out_hbm, w_out),
                (w_long_hbm, w_long),
                (w_in_hbm, w_in),
                (state_hbm, state),
                (cosine_hbm, cosine),
                (sunlit_hbm, sunlit),
                (table_hbm, table),
                (quad_hbm, quad),
                (fourier_hbm, fourier),
                (legendre_hbm, legendre),
                (damping_hbm, damping),
            )
        )
    ]
    for load in loads[:6]:
        load.start()

    band = lax.axis_index("band")
    field = lax.axis_index("field")
    x, y, core = band // 8, lax.rem(band // 2, 4), lax.rem(band, 2)

    bands = [
        lax.rem(x + i, 4) * 8 + lax.rem(y + j, 4) * 2 + lax.rem(core + k, 2)
        for i, j in ((2, 2), (2, 1), (2, 3), (1, 2), (3, 2), (2, 0), (0, 2), (1, 1), (1, 3), (3, 1))
        + ((3, 3), (1, 0), (3, 0), (0, 1), (0, 3), (0, 0))
        for k in (1, 0)
    ]

    def ring(start, stop, act):
        def one_field(t, carry):
            near = (t + 1) // 2
            other = lax.rem(field + 12 + near * (1 - 2 * lax.rem(t, 2)), 8)
            for other_band in bands:
                act(other_band, other)
            return carry

        lax.fori_loop(start, stop, one_field, 0)

    fields = [lax.rem(field + i, 8) for i in (4, 3, 5, 2, 6, 1, 7)]

    def plane(act):
        for other_band in bands[:-1]:
            act(other_band, field)

    barrier = pltpu.get_barrier_semaphore()

    def greet(other_band, other_field):
        pl.semaphore_signal(
            barrier, inc=1, device_id=(other_band, other_field), device_id_type=MESH
        )

    for other_field in fields:
        for other_band in bands:
            greet(other_band, other_field)
    plane(greet)

    def exchange_band(source, target, slot):
        def one(other_band, other_field):
            pltpu.make_async_remote_copy(
                src_ref=source.at[other_band], dst_ref=target.at[band],
                send_sem=send_sems.at[slot], recv_sem=recv_sems.at[slot],
                device_id=(other_band, other_field), device_id_type=MESH,
            ).start()

        plane(one)
        target[band] = source[band]

    def arrived(target, slot, count):
        part = target.at[pl.ds(0, count)]
        pltpu.make_async_copy(part, part, recv_sems.at[slot]).wait()

    def gone(source, slot, count):
        part = source.at[pl.ds(0, count)]
        pltpu.make_async_copy(part, part, send_sems.at[slot]).wait()

    loads[0].wait()
    loads[1].wait()
    out_t[...] = (nt(eye(128), w_out[...]) * 0.5).astype(BF16)
    in_t[2048:, :] = nt(eye(128), w_long[...]).astype(BF16)
    loads[2].wait()
    for h in range(0, 2048, 256):
        in_t[h : h + 256, :] = nt(eye(256), w_in[:, h : h + 256]).astype(BF16)
    loads[3].wait()
    for load in loads[6:]:
        load.start()
    for h in range(0, 2048, HCHUNK):
        hidden[h : h + HCHUNK, :] = gelu2(nt(in_t[h : h + HCHUNK, :], state[...]))
    long_wave[...] = nt(in_t[2048:, :], state[...])
    loads[4].wait()
    loads[5].wait()
    light = sunlit[...].astype(F32) * cosine[...]
    light = jnp.concatenate([light[0:1, :], light[1:2, :]], axis=1)
    for c in range(0, 2560, CHUNK):
        here = slice(c, c + CHUNK)
        short = nn(out_t[...], hidden[:, here]).astype(BF16).astype(F32)
        heat_t[:, here] = (long_wave[:, here] + light[:, here] * short).astype(BF16)

    loads[6].wait()
    loads[7].wait()
    lane = lax.broadcasted_iota(jnp.int32, (32, 128), 1)
    pieces = []
    rows = jnp.concatenate([table[i] for i in range(10)], axis=1)
    for row in range(2):
        both = nt(rows, heat_t[:, row * LON : (row + 1) * LON])
        weight = quad[field * 2 + row]
        pieces += [(both[i : i + 32, :] + both[i + 64 : i + 96, :]) * weight for i in (0, 32)]
    for z in range(8):
        block = jnp.zeros((32, 128), F32)
        for k in range(4):
            moved = pltpu.roll(pieces[k], (16 * (k - z)) % 128, 1)
            block = jnp.where(lane // 16 == k, moved, block)
        sent_all[z * 32 : (z + 1) * 32, :] = block

    mine = pl.ds(band * 8 + lax.rem(field, 4) * 2 + field // 4, 1)

    def send_heat(other_band, other_field):
        pltpu.make_async_remote_copy(
            src_ref=sent_all.at[pl.ds(other_field * 32 + other_band, 1)], dst_ref=got_all.at[mine],
            send_sem=send_sems.at[0], recv_sem=recv_sems.at[0],
            device_id=(other_band, other_field), device_id_type=MESH,
        ).start()

    pl.semaphore_wait(barrier, 255)
    ring(0, 7, send_heat)
    plane(send_heat)
    got_all[mine, :] = sent_all[pl.ds(field * 32 + band, 1), :]

    loads[8].wait()
    waves = nt(eye(32), fourier[...])
    for l in range(16):
        j = place(l // 2) * 2 + l % 2
        trans[pl.ds(j, 32, stride=16), :] = waves[:, l * 128 : (l + 1) * 128] * quad[l]
    send1[...] = trans[...].astype(BF16).reshape(32, 16, 128)
    exchange_band(send1, recv1, 1)

    loads[9].wait()
    loads[10].wait()

    def latitude(order):
        spot = order % 8
        return order % 256 // 8 * 16 + (spot % 2 * 4 + spot // 2) * 2 + order // 256

    down = lax.broadcasted_iota(jnp.int32, (512, 512), 0)
    across = lax.broadcasted_iota(jnp.int32, (512, 512), 1)
    leg_p[...] = nn(legendre[...], (down == latitude(across)).astype(BF16)).astype(BF16)
    leg_t[...] = nt((across == latitude(down)).astype(BF16), legendre[...]).astype(BF16)
    for j in range(5):
        column = jnp.broadcast_to(damping[:, j * 128 : (j + 1) * 128], (128, 128))
        damp[j * 128 : (j + 1) * 128, :] = column.T
    for j in range(0, 2560, 256):
        heating[j : j + 256, :] = heat_t[:, j : j + 256].astype(F32).T.astype(BF16)

    arrived(recv1, 1, 31)
    trans[...] = recv1[...].reshape(512, 128).astype(F32)
    lane = lax.broadcasted_iota(jnp.int32, (256, 128), 1)
    cool = jnp.zeros((256, 128), F32)
    for row in range(2):
        half = trans[pl.ds(row, 256, stride=2), :]
        tall[row * 256 : (row + 1) * 256, :] = half.astype(BF16)
        for part in range(2):
            k = row * 2 + part
            moved = pltpu.roll(half, (16 * k - 64 * part - 32) % 128, 1)
            cool = jnp.where(lane // 16 == k, moved, cool)
    wide[...] = cool
    damped = (nn(leg_p[...], tall[...]) * damp[...]).astype(BF16)
    out = nn(leg_t[...], damped)
    for row in range(2):
        trans[pl.ds(row, 256, stride=2), :] = out[row * 256 : (row + 1) * 256, :]
    back1[...] = trans[...].astype(BF16).reshape(32, 16, 128)
    exchange_band(back1, home1, 2)

    arrived(got_all, 0, 255)
    warm = wide[...] + got_all[...]
    tall[:256, :] = warm.astype(BF16)
    tall[256:, :] = pltpu.roll(warm, 96, 1).astype(BF16)
    damped = (nn(leg_p[...], tall[...]) * damp[...]).astype(BF16)
    out = nn(leg_t[...], damped)
    wide[...] = jnp.where(lane < 32, out[:256, :], pltpu.roll(out[256:, :], 32, 1))
    pair = jnp.where(
        lane[:128, :] < 64,
        wide[pl.ds(0, 128, stride=2), :],
        pltpu.roll(wide[pl.ds(1, 128, stride=2), :], 64, 1),
    )
    back2[...] = pair.astype(BF16).reshape(32, 4, 128)
    exchange_band(back2, home2, 3)

    arrived(home1, 2, 31)
    trans[...] = home1[...].reshape(512, 128).astype(F32)
    for l in range(16):
        j = place(l // 2) * 2 + l % 2
        piece = trans[pl.ds(j, 32, stride=16), :].T
        updated[l // 2, l % 2] = piece.astype(BF16).reshape(2, 4, 16, 32)
    arrived(home2, 3, 31)
    wide[:128, :] = home2[...].reshape(128, 128).astype(F32)
    for low in range(4):
        piece = wide[pl.ds(low, 32, stride=4), :].T.astype(BF16).reshape(2, 2, 2, 16, 32)
        for high in range(2):
            updated[high * 4 + low, :, :, 2] = piece[high]

    gone(got_all, 0, 255)
    gone(send1, 1, 31)
    gone(back1, 2, 31)
    gone(back2, 3, 31)


def finish(heating, updated, heating_out, updated_out, sems):
    copies = []
    for i in range(4):
        part = pl.ds(i * 640, 640)
        copies.append(pltpu.make_async_copy(heating.at[part], heating_out.at[part], sems.at[i]))
    for i in range(2):
        part = pl.ds(i * 4, 4)
        copies.append(pltpu.make_async_copy(updated.at[part], updated_out.at[part], sems.at[4 + i]))
    for copy in copies:
        copy.start()
    for copy in copies:
        copy.wait()


def local(
    column_state, cosine, sunlit, w_in, w_out, w_long, fourier, quadrature, legendre, damping
):
    hbm = pl.BlockSpec(memory_space=pltpu.HBM)
    vmem = pl.BlockSpec(memory_space=pltpu.VMEM)
    anywhere = pl.BlockSpec(memory_space=pl.ANY)
    operands = (
        column_state.reshape(2560, 256),
        cosine,
        sunlit,
        w_in,
        w_out,
        w_long,
        jnp.asarray(fourier_rows()),
        fourier.transpose(0, 2, 3, 4, 1).reshape(2048, 32),
        quadrature,
        legendre.reshape(640, 512),
        damping,
    )
    held = [pltpu.VMEM(x.shape, x.dtype) for x in operands]
    held[8] = pltpu.SMEM((16,), F32)
    whole = pltpu.VMEM((32, 16, 128), BF16)
    small = pltpu.VMEM((32, 4, 128), BF16)
    heating, updated = pl.pallas_call(
        kernel,
        out_shape=(
            pltpu.VMEM((2560, 128), BF16),
            pltpu.VMEM((8, 2, 2, 4, 16, 32), BF16),
        ),
        in_specs=[hbm] * len(operands),
        out_specs=(vmem, vmem),
        scratch_shapes=held
        + [
            pltpu.VMEM((2176, 256), BF16),
            pltpu.VMEM((128, 2048), BF16),
            pltpu.VMEM((2048, 2560), BF16),
            pltpu.VMEM((128, 2560), F32),
            pltpu.VMEM((128, 2560), BF16),
            pltpu.VMEM((256, 128), F32),
            pltpu.VMEM((256, 128), F32),
            whole, whole, whole, whole,
            small, small,
            pltpu.VMEM((512, 128), F32),
            pltpu.VMEM((512, 128), BF16),
            pltpu.VMEM((256, 128), F32),
            pltpu.VMEM((640, 512), BF16),
            pltpu.VMEM((512, 640), BF16),
            pltpu.VMEM((640, 128), F32),
            pltpu.SemaphoreType.DMA((len(operands),)),
            pltpu.SemaphoreType.DMA((4,)),
            pltpu.SemaphoreType.DMA((4,)),
        ],
        compiler_params=pltpu.CompilerParams(
            collective_id=0, has_side_effects=True, vmem_limit_bytes=48 * 2**20
        ),
        name="step",
    )(*[pltpu.with_memory_space_constraint(x, pltpu.HBM) for x in operands])
    heating, updated = pl.pallas_call(
        finish,
        out_shape=(
            jax.ShapeDtypeStruct((2560, 128), BF16),
            jax.ShapeDtypeStruct((8, 2, 2, 4, 16, 32), BF16),
        ),
        in_specs=[anywhere] * 2,
        out_specs=(anywhere, anywhere),
        scratch_shapes=[pltpu.SemaphoreType.DMA((6,))],
        compiler_params=pltpu.CompilerParams(vmem_limit_bytes=FINISH_VMEM),
        name="finish",
    )(heating, updated)
    updated = updated.reshape(16, 2, 4, 16, 32).transpose(0, 4, 1, 2, 3)
    return heating.reshape(2, 1280, 128), updated


def solution(mesh):
    in_specs = (
        P(("band", "field"), None, None),
        P(("band", "field"), None),
        P(("band", "field"), None),
        P(),
        P(),
        P(),
        P("band", None, None, None, "field"),
        P("band"),
        P("band", None, None),
        P("band", None),
    )
    out_specs = (P(("band", "field"), None, None), P("band", None, None, None, "field"))
    return jax.shard_map(local, mesh=mesh, in_specs=in_specs, out_specs=out_specs, check_vma=False)
```

```python
import jax
import jax.numpy as jnp
import ml_dtypes
import numpy as np
from jax import lax
from jax.experimental import pallas as pl
from jax.experimental.pallas import tpu as pltpu
from jax.sharding import PartitionSpec as P

F32 = jnp.float32
BF16 = jnp.bfloat16
LON = 1280
WAVES = 32
HCHUNK = 512
CHUNK = 256
ALL_VMEM = 64 * 2**20 - 65536
FINISH_VMEM = 2**20
MESH = pl.DeviceIdType.MESH
GELU_A = 0.7978845608028654
GELU_B = 0.7978845608028654 * 0.044715


def nt(a, b):
    return lax.dot_general(a, b, (((1,), (1,)), ((), ())), preferred_element_type=F32)


def nn(a, b):
    return jnp.dot(a, b, preferred_element_type=F32)


def place(z):
    return (z % 4) * 2 + z // 4


def fourier_rows():
    phase = np.arange(LON)[None, :] * np.arange(WAVES)[:, None] % LON
    angle = 2.0 * np.pi / LON * phase
    full = np.stack([np.cos(angle), -np.sin(angle)]) / np.sqrt(LON)
    high = full.astype(ml_dtypes.bfloat16)
    low = (full - high.astype(np.float64)).astype(ml_dtypes.bfloat16)
    return np.stack([high, low]).reshape(4 * WAVES, 10, 128).swapaxes(0, 1).copy()


def gelu2(x):
    x = x.astype(BF16)
    inner = x * (x * x * BF16(GELU_B) + BF16(GELU_A))
    return x + x * jnp.tanh(inner)


def eye(n):
    row = lax.broadcasted_iota(jnp.int32, (n, n), 0)
    return (row == lax.broadcasted_iota(jnp.int32, (n, n), 1)).astype(BF16)


def kernel(
    state_hbm, cosine_hbm, sunlit_hbm, w_in_hbm, w_out_hbm, w_long_hbm, table_hbm,
    fourier_hbm, quad_hbm, legendre_hbm, damping_hbm,
    heating, updated,
    state, cosine, sunlit, w_in, w_out, w_long, table, fourier, quad, legendre, damping,
    in_t, out_t, hidden, long_wave, heat_t, sent_all, got_all,
    send1, recv1, back1, home1, back2, home2,
    trans, tall, wide, leg_p, leg_t, damp, load_sems, send_sems, recv_sems,
):
    loads = [
        pltpu.make_async_copy(source, target, load_sems.at[i])
        for i, (source, target) in enumerate(
            (
                (w_out_hbm, w_out),
                (w_long_hbm, w_long),
                (w_in_hbm, w_in),
                (state_hbm, state),
                (cosine_hbm, cosine),
                (sunlit_hbm, sunlit),
                (table_hbm, table),
                (quad_hbm, quad),
                (fourier_hbm, fourier),
                (legendre_hbm, legendre),
                (damping_hbm, damping),
            )
        )
    ]
    for load in loads[:6]:
        load.start()

    band = lax.axis_index("band")
    field = lax.axis_index("field")
    x, y, core = band // 8, lax.rem(band // 2, 4), lax.rem(band, 2)

    bands = [
        lax.rem(x + i, 4) * 8 + lax.rem(y + j, 4) * 2 + lax.rem(core + k, 2)
        for i, j in ((2, 2), (2, 1), (2, 3), (1, 2), (3, 2), (2, 0), (0, 2), (1, 1), (1, 3), (3, 1))
        + ((3, 3), (1, 0), (3, 0), (0, 1), (0, 3), (0, 0))
        for k in (1, 0)
    ]

    def ring(start, stop, act):
        def one_field(t, carry):
            near = (t + 1) // 2
            other = lax.rem(field + 12 + near * (1 - 2 * lax.rem(t, 2)), 8)
            for other_band in bands:
                act(other_band, other)
            return carry

        lax.fori_loop(start, stop, one_field, 0)

    fields = [lax.rem(field + i, 8) for i in (4, 3, 5, 2, 6, 1, 7)]

    def plane(act):
        for other_band in bands[:-1]:
            act(other_band, field)

    barrier = pltpu.get_barrier_semaphore()

    def greet(other_band, other_field):
        pl.semaphore_signal(
            barrier, inc=1, device_id=(other_band, other_field), device_id_type=MESH
        )

    for other_field in fields:
        for other_band in bands:
            greet(other_band, other_field)
    plane(greet)

    def exchange_band(source, target, slot):
        def one(other_band, other_field):
            pltpu.make_async_remote_copy(
                src_ref=source.at[other_band], dst_ref=target.at[band],
                send_sem=send_sems.at[slot], recv_sem=recv_sems.at[slot],
                device_id=(other_band, other_field), device_id_type=MESH,
            ).start()

        plane(one)
        target[band] = source[band]

    def arrived(target, slot, count):
        part = target.at[pl.ds(0, count)]
        pltpu.make_async_copy(part, part, recv_sems.at[slot]).wait()

    def gone(source, slot, count):
        part = source.at[pl.ds(0, count)]
        pltpu.make_async_copy(part, part, send_sems.at[slot]).wait()

    for load in loads[:4]:
        load.wait()
    for load in loads[6:]:
        load.start()
    for h in range(0, 2048, HCHUNK):
        for i in range(h, h + HCHUNK, 256):
            in_t[i : i + 256, :] = nt(eye(256), w_in[:, i : i + 256]).astype(BF16)
        hidden[h : h + HCHUNK, :] = gelu2(nt(in_t[h : h + HCHUNK, :], state[...]))
    in_t[2048:, :] = nt(eye(128), w_long[...]).astype(BF16)
    out_t[...] = (nt(eye(128), w_out[...]) * 0.5).astype(BF16)
    long_wave[...] = nt(in_t[2048:, :], state[...])
    loads[4].wait()
    loads[5].wait()
    light = sunlit[...].astype(F32) * cosine[...]
    light = jnp.concatenate([light[0:1, :], light[1:2, :]], axis=1)
    for c in range(0, 2560, CHUNK):
        here = slice(c, c + CHUNK)
        short = nn(out_t[...], hidden[:, here]).astype(BF16).astype(F32)
        heat_t[:, here] = (long_wave[:, here] + light[:, here] * short).astype(BF16)

    loads[6].wait()
    loads[7].wait()
    lane = lax.broadcasted_iota(jnp.int32, (32, 128), 1)
    pieces = []
    rows = jnp.concatenate([table[i] for i in range(10)], axis=1)
    for row in range(2):
        both = nt(rows, heat_t[:, row * LON : (row + 1) * LON])
        weight = quad[field * 2 + row]
        pieces += [(both[i : i + 32, :] + both[i + 64 : i + 96, :]) * weight for i in (0, 32)]
    for z in range(8):
        block = jnp.zeros((32, 128), F32)
        for k in range(4):
            moved = pltpu.roll(pieces[k], (16 * (k - z)) % 128, 1)
            block = jnp.where(lane // 16 == k, moved, block)
        sent_all[z * 32 : (z + 1) * 32, :] = block

    mine = pl.ds(band * 8 + lax.rem(field, 4) * 2 + field // 4, 1)

    def send_heat(other_band, other_field):
        pltpu.make_async_remote_copy(
            src_ref=sent_all.at[pl.ds(other_field * 32 + other_band, 1)], dst_ref=got_all.at[mine],
            send_sem=send_sems.at[0], recv_sem=recv_sems.at[0],
            device_id=(other_band, other_field), device_id_type=MESH,
        ).start()

    pl.semaphore_wait(barrier, 255)
    ring(0, 7, send_heat)
    plane(send_heat)
    got_all[mine, :] = sent_all[pl.ds(field * 32 + band, 1), :]

    loads[8].wait()
    waves = nt(eye(32), fourier[...])
    for l in range(16):
        j = place(l // 2) * 2 + l % 2
        trans[pl.ds(j, 32, stride=16), :] = waves[:, l * 128 : (l + 1) * 128] * quad[l]
    send1[...] = trans[...].astype(BF16).reshape(32, 16, 128)
    exchange_band(send1, recv1, 1)

    loads[9].wait()
    loads[10].wait()

    def latitude(order):
        spot = order % 8
        return order % 256 // 8 * 16 + (spot % 2 * 4 + spot // 2) * 2 + order // 256

    down = lax.broadcasted_iota(jnp.int32, (512, 512), 0)
    across = lax.broadcasted_iota(jnp.int32, (512, 512), 1)
    leg_p[...] = nn(legendre[...], (down == latitude(across)).astype(BF16)).astype(BF16)
    leg_t[...] = nt((across == latitude(down)).astype(BF16), legendre[...]).astype(BF16)
    for j in range(5):
        column = jnp.broadcast_to(damping[:, j * 128 : (j + 1) * 128], (128, 128))
        damp[j * 128 : (j + 1) * 128, :] = column.T
    for j in range(0, 2560, 256):
        heating[j : j + 256, :] = heat_t[:, j : j + 256].astype(F32).T.astype(BF16)

    arrived(recv1, 1, 31)
    trans[...] = recv1[...].reshape(512, 128).astype(F32)
    lane = lax.broadcasted_iota(jnp.int32, (256, 128), 1)
    cool = jnp.zeros((256, 128), F32)
    for row in range(2):
        half = trans[pl.ds(row, 256, stride=2), :]
        tall[row * 256 : (row + 1) * 256, :] = half.astype(BF16)
        for part in range(2):
            k = row * 2 + part
            moved = pltpu.roll(half, (16 * k - 64 * part - 32) % 128, 1)
            cool = jnp.where(lane // 16 == k, moved, cool)
    wide[...] = cool
    damped = (nn(leg_p[...], tall[...]) * damp[...]).astype(BF16)
    out = nn(leg_t[...], damped)
    for row in range(2):
        trans[pl.ds(row, 256, stride=2), :] = out[row * 256 : (row + 1) * 256, :]
    back1[...] = trans[...].astype(BF16).reshape(32, 16, 128)
    exchange_band(back1, home1, 2)

    arrived(got_all, 0, 255)
    warm = wide[...] + got_all[...]
    tall[:256, :] = warm.astype(BF16)
    tall[256:, :] = pltpu.roll(warm, 96, 1).astype(BF16)
    damped = (nn(leg_p[...], tall[...]) * damp[...]).astype(BF16)
    out = nn(leg_t[...], damped)
    wide[...] = jnp.where(lane < 32, out[:256, :], pltpu.roll(out[256:, :], 32, 1))
    pair = jnp.where(
        lane[:128, :] < 64,
        wide[pl.ds(0, 128, stride=2), :],
        pltpu.roll(wide[pl.ds(1, 128, stride=2), :], 64, 1),
    )
    back2[...] = pair.astype(BF16).reshape(32, 4, 128)
    exchange_band(back2, home2, 3)

    arrived(home1, 2, 31)
    trans[...] = home1[...].reshape(512, 128).astype(F32)
    for l in range(16):
        j = place(l // 2) * 2 + l % 2
        piece = trans[pl.ds(j, 32, stride=16), :].T
        updated[l // 2, l % 2] = piece.astype(BF16).reshape(2, 4, 16, 32)
    arrived(home2, 3, 31)
    wide[:128, :] = home2[...].reshape(128, 128).astype(F32)
    for low in range(4):
        piece = wide[pl.ds(low, 32, stride=4), :].T.astype(BF16).reshape(2, 2, 2, 16, 32)
        for high in range(2):
            updated[high * 4 + low, :, :, 2] = piece[high]

    gone(got_all, 0, 255)
    gone(send1, 1, 31)
    gone(back1, 2, 31)
    gone(back2, 3, 31)


def finish(heating, updated, heating_out, updated_out, sems):
    copies = []
    for i in range(1):
        part = pl.ds(i * 2560, 2560)
        copies.append(pltpu.make_async_copy(heating.at[part], heating_out.at[part], sems.at[i]))
    for i in range(1):
        part = pl.ds(i * 8, 8)
        copies.append(pltpu.make_async_copy(updated.at[part], updated_out.at[part], sems.at[1 + i]))
    for copy in copies:
        copy.start()
    for copy in copies:
        copy.wait()


def local(
    column_state, cosine, sunlit, w_in, w_out, w_long, fourier, quadrature, legendre, damping
):
    hbm = pl.BlockSpec(memory_space=pltpu.HBM)
    vmem = pl.BlockSpec(memory_space=pltpu.VMEM)
    anywhere = pl.BlockSpec(memory_space=pl.ANY)
    operands = (
        column_state.reshape(2560, 256),
        cosine,
        sunlit,
        w_in,
        w_out,
        w_long,
        jnp.asarray(fourier_rows()),
        fourier.transpose(0, 2, 3, 4, 1).reshape(2048, 32),
        quadrature,
        legendre.reshape(640, 512),
        damping,
    )
    held = [pltpu.VMEM(x.shape, x.dtype) for x in operands]
    held[8] = pltpu.SMEM((16,), F32)
    whole = pltpu.VMEM((32, 16, 128), BF16)
    small = pltpu.VMEM((32, 4, 128), BF16)
    heating, updated = pl.pallas_call(
        kernel,
        out_shape=(
            pltpu.VMEM((2560, 128), BF16),
            pltpu.VMEM((8, 2, 2, 4, 16, 32), BF16),
        ),
        in_specs=[hbm] * len(operands),
        out_specs=(vmem, vmem),
        scratch_shapes=held
        + [
            pltpu.VMEM((2176, 256), BF16),
            pltpu.VMEM((128, 2048), BF16),
            pltpu.VMEM((2048, 2560), BF16),
            pltpu.VMEM((128, 2560), F32),
            pltpu.VMEM((128, 2560), BF16),
            pltpu.VMEM((256, 128), F32),
            pltpu.VMEM((256, 128), F32),
            whole, whole, whole, whole,
            small, small,
            pltpu.VMEM((512, 128), F32),
            pltpu.VMEM((512, 128), BF16),
            pltpu.VMEM((256, 128), F32),
            pltpu.VMEM((640, 512), BF16),
            pltpu.VMEM((512, 640), BF16),
            pltpu.VMEM((640, 128), F32),
            pltpu.SemaphoreType.DMA((len(operands),)),
            pltpu.SemaphoreType.DMA((4,)),
            pltpu.SemaphoreType.DMA((4,)),
        ],
        compiler_params=pltpu.CompilerParams(
            collective_id=0, has_side_effects=True, vmem_limit_bytes=48 * 2**20
        ),
        name="step",
    )(*[pltpu.with_memory_space_constraint(x, pltpu.HBM) for x in operands])
    heating, updated = pl.pallas_call(
        finish,
        out_shape=(
            jax.ShapeDtypeStruct((2560, 128), BF16),
            jax.ShapeDtypeStruct((8, 2, 2, 4, 16, 32), BF16),
        ),
        in_specs=[anywhere] * 2,
        out_specs=(anywhere, anywhere),
        scratch_shapes=[pltpu.SemaphoreType.DMA((2,))],
        compiler_params=pltpu.CompilerParams(vmem_limit_bytes=FINISH_VMEM),
        name="finish",
    )(heating, updated)
    updated = updated.reshape(16, 2, 4, 16, 32).transpose(0, 4, 1, 2, 3)
    return heating.reshape(2, 1280, 128), updated


def solution(mesh):
    in_specs = (
        P(("band", "field"), None, None),
        P(("band", "field"), None),
        P(("band", "field"), None),
        P(),
        P(),
        P(),
        P("band", None, None, None, "field"),
        P("band"),
        P("band", None, None),
        P("band", None),
    )
    out_specs = (P(("band", "field"), None, None), P("band", None, None, None, "field"))
    return jax.shard_map(local, mesh=mesh, in_specs=in_specs, out_specs=out_specs, check_vma=False)
```
